32 devices in a mesh: pole: 2 (over x), prow: 16 (over z, y, core).
Axes of the slice: x: 2, y: 2, z: 4, core: 2. Of those that a mesh axis runs over, the one named last changes fastest.
Arguments:
- inverse_window: bfloat16 [8192, 4096], P(('pole', 'prow')), parts along dimension 0, may hold values from -8 to 8, as said below
- panel_one: bfloat16 [8192, 256], P(('pole', 'prow')), parts along dimension 0, may hold values from -0.09375 to 0.09375
- panel_two: bfloat16 [8192, 256], P(('pole', 'prow')), parts along dimension 0, may hold values from -0.09375 to 0.09375
- cross_block: bfloat16 [512, 256], P('pole'), parts along dimension 0, may hold values from -0.375 to 0.375
- diag_one: float32 [512, 256], P('pole'), parts along dimension 0, may hold values from -6 to 6
- diag_two: float32 [512, 256], P('pole'), parts along dimension 0, may hold values from -6 to 6
- row_super: int32 [4096], P('prow'), may hold values from 0 to 15, as said below
- struct_mask: int32 [2, 16], replicated, may hold values from 0 to 1, as said below
Outputs:
- column_one: bfloat16 [8192, 256], P(('pole', 'prow')), parts along dimension 0
- block_one: float32 [512, 256], P('pole'), parts along dimension 0
- column_two: bfloat16 [8192, 256], P(('pole', 'prow')), parts along dimension 0
- edge_block: float32 [512, 256], P('pole'), parts along dimension 0
- block_two: float32 [512, 256], P('pole'), parts along dimension 0
The draws below stay inside these ranges and needn't reach their ends.
There are 2 independent parts, one for each index of `pole`. The reference program is written for one: setup_inputs(seed, part) draws one part's arguments, and reference() takes and returns one part's arrays. A program takes and returns all parts, laid end to end along the dimension named above; an argument that names none is the same for every part. Nothing has to cross between parts.
Inputs may be any that keep to these rules, and one draw needn't show every extreme that they name: `inverse_window`: symmetric. `row_super`: never falling; each ancestor supernode covers 256 // 2 to 384 consecutive rows, and one covers exactly 384. `struct_mask`: each aligned block of 256 window rows holds a row whose supernode lies in both structures.
All inputs are finite; a program needn't handle non-finite values.
Results may differ from the reference program's by a relative error of at most 0.0041.
Values may be sent and summed in bfloat16 or wider, within the bound.
No kernel may reach another device: no remote copies, remote signals or barrier semaphores. Data moves between devices by JAX's collectives and lax.ppermute only.
A program may use at most 128 MiB of HBM per device.

```python
import jax
import jax.numpy as jnp
from jax import lax

SN = 256
SUPW = 256
ROWS_DEV = 256
WIN = 4096
NSEG = 16


def draw_inverse_window(key, part):
    key = jax.random.fold_in(key, 11)
    first = jax.random.fold_in(key, 0)
    base = jax.random.normal(first, (WIN, WIN), jnp.float32)
    sym = (base + base.T) * 0.70710678
    return jnp.clip(sym, -8.0, 8.0).astype(jnp.bfloat16)


def segment_rows(key):
    key = jax.random.fold_in(key, 5)
    first, second = jax.random.split(key)
    pairs = NSEG // 2
    shifts = jax.random.randint(first, (pairs,), -(SUPW // 2), SUPW // 2 + 1)
    chosen = jax.random.randint(second, (), 0, pairs)
    shifts = jnp.where(jnp.arange(pairs, dtype=jnp.int32) == chosen, SUPW // 2, shifts)
    lengths = jnp.stack([SUPW + shifts, SUPW - shifts], axis=1).reshape(NSEG)
    ends = jnp.cumsum(lengths).astype(jnp.int32)
    rows = jnp.arange(WIN, dtype=jnp.int32)
    return jnp.sum((rows[:, None] >= ends[None, :]).astype(jnp.int32), axis=1).astype(jnp.int32)


def draw_row_super(key, part):
    return segment_rows(key)


def draw_struct_mask(key, part):
    segs = segment_rows(key)
    key = jax.random.fold_in(key, 17)
    first, second = jax.random.split(key)
    bits = jax.random.randint(first, (2, NSEG), 0, 2)
    blocks = WIN // ROWS_DEV
    picks = jnp.arange(blocks, dtype=jnp.int32) * ROWS_DEV + jax.random.randint(second, (blocks,), 0, ROWS_DEV)
    chosen = segs[picks]
    forced = jnp.max((chosen[:, None] == jnp.arange(NSEG, dtype=jnp.int32)[None, :]).astype(jnp.int32), axis=0)
    return jnp.maximum(bits, forced[None, :]).astype(jnp.int32)


def levels(rng, shape, shards, low, top_value):
    factor_of = 1.0
    for dim, shards_of in shards:
        heights = jax.random.uniform(jax.random.fold_in(jax.random.fold_in(rng, 6), dim), (shards_of,), jnp.float32, low / len(shards), top_value / len(shards))
        factor_of = factor_of * jnp.repeat(jnp.exp(heights), shape[dim] // shards_of).reshape((-1,) + (1,) * (len(shape) - 1 - dim))
    return factor_of


def gaussian(rng, dims, deviation, reach, cuts=(), kind=jnp.bfloat16):
    drawn = jax.random.normal(rng, dims, jnp.float32) * deviation
    if len(cuts) > 0:
        drawn = levels(rng, dims, cuts, -0.22, 0.18) * drawn
    return jnp.clip(drawn, min=-reach, max=reach).astype(kind)


def setup_inputs(seed: int = 0, part: int = 0) -> dict:
    keys = jax.random.split(jax.random.key(seed), 9)
    part_splits = jax.random.split(jax.random.fold_in(keys[8], part), 9)
    inverse_window = draw_inverse_window(jax.random.fold_in(jax.random.fold_in(keys[8], part), 71), part)
    panel_one = gaussian(part_splits[1], (WIN, SN), WIN ** -0.5, 0.09375, ((0, 16),))
    panel_two = gaussian(part_splits[2], (WIN, SN), WIN ** -0.5, 0.09375, ((0, 16),))
    cross_block = gaussian(part_splits[3], (SN, SN), SN ** -0.5, 0.375)
    diag_one = gaussian(part_splits[4], (SN, SN), 1.0, 6.0, (), jnp.float32)
    diag_two = gaussian(part_splits[5], (SN, SN), 1.0, 6.0, (), jnp.float32)
    row_super = draw_row_super(jax.random.fold_in(keys[8], 71), part)
    struct_mask = draw_struct_mask(jax.random.fold_in(keys[8], 71), part)
    return dict(inverse_window=inverse_window, panel_one=panel_one, panel_two=panel_two, cross_block=cross_block, diag_one=diag_one, diag_two=diag_two, row_super=row_super, struct_mask=struct_mask)


def lookup(row_super, table):
    return jnp.take(table, row_super).astype(jnp.float32)


def reference(inverse_window, panel_one, panel_two, cross_block, diag_one, diag_two, row_super, struct_mask):
    highest = lax.Precision.HIGHEST
    weight_one = lookup(row_super, struct_mask[0])
    weight_two = lookup(row_super, struct_mask[1])
    masked_one = (panel_one.astype(jnp.float32) * weight_one[:, None]).astype(jnp.bfloat16)
    masked_two = (panel_two.astype(jnp.float32) * weight_two[:, None]).astype(jnp.bfloat16)
    image_one = jnp.dot(inverse_window, masked_one, preferred_element_type=jnp.float32)
    exact_one = -(weight_one[:, None] * image_one)
    schur_one = jnp.dot(masked_one.astype(jnp.float32).T, exact_one, precision=highest)
    block_one = diag_one - schur_one
    column_one = exact_one.astype(jnp.bfloat16)
    image_two = jnp.dot(inverse_window, masked_two, preferred_element_type=jnp.float32)
    carried = jnp.dot(column_one, cross_block, preferred_element_type=jnp.float32)
    exact_two = -(weight_two[:, None] * (image_two + carried))
    cross_sum = jnp.dot(masked_two.T, column_one, preferred_element_type=jnp.float32)
    cross_wide = cross_block.astype(jnp.float32)
    edge_block = -(cross_sum.T + jnp.dot(block_one, cross_wide, precision=highest))
    schur_two = jnp.dot(masked_two.astype(jnp.float32).T, exact_two, precision=highest)
    block_two = diag_two - schur_two - jnp.dot(cross_wide.T, edge_block, precision=highest)
    return column_one, block_one, exact_two.astype(jnp.bfloat16), edge_block, block_two
```

```python
import functools

import jax
import jax.numpy as jnp
from jax import lax
from jax.experimental import pallas as pl
from jax.experimental.pallas import tpu as pltpu
from jax.sharding import PartitionSpec as P

F32, BF16 = jnp.float32, jnp.bfloat16
AXIS = "prow"
VMEM = pl.BlockSpec(memory_space=pltpu.VMEM)
SMEM = pl.BlockSpec(memory_space=pltpu.SMEM)


def dot(left, right):
    return jnp.dot(left, right, preferred_element_type=F32)


def dot_t(left, right):
    return lax.dot_general(left, right, (((0,), (0,)), ((), ())), preferred_element_type=F32)


def halves(x):
    high = x.astype(BF16)
    return high, (x - high.astype(F32)).astype(BF16)


def call(body, name, outs, args, n_smem=0, flops=0):
    size = sum(a.size * a.dtype.itemsize for a in args)
    return pl.pallas_call(
        body,
        name=name,
        out_shape=tuple(jax.ShapeDtypeStruct(s, d) for s, d in outs),
        in_specs=[SMEM] * n_smem + [VMEM] * (len(args) - n_smem),
        out_specs=tuple(VMEM for _ in outs),
        compiler_params=pltpu.CompilerParams(vmem_limit_bytes=32 << 20),
        cost_estimate=pl.CostEstimate(flops=flops, bytes_accessed=size, transcendentals=0),
    )(*args)


def mask_body(table, rows, one, two, m_one, m_two, w_one, w_two):
    n = one.shape[0]
    index = rows[...]
    on_diagonal = lax.broadcasted_iota(jnp.int32, (n, n), 0) == lax.broadcasted_iota(jnp.int32, (n, n), 1)
    ones = jnp.ones((n, n), BF16)
    for which, panel, masked, weights in ((0, one, m_one, w_one), (1, two, m_two, w_two)):
        weight = jnp.zeros(index.shape, F32)
        for s in range(table.shape[1]):
            weight = jnp.where(index == s, table[which, s].astype(F32), weight)
        chosen = jnp.where(on_diagonal, jnp.broadcast_to(weight, (n, n)), 0.0).astype(BF16)
        masked[...] = dot(chosen, panel[...]).astype(BF16)
        weights[...] = dot(chosen, ones).astype(BF16)


def swap_body(place, window, out):
    width = out.shape[0]
    other = 1 - place[0]
    for t in range(out.shape[1] // width):
        out[:, t * width : (t + 1) * width] = window[:, pl.ds((2 * t + other) * width, width)]


def image_body(place, window, swapped, mine, sibling, *rest):
    pieces, (own, other, total) = rest[:-3], rest[-3:]
    n = mine.shape[0]
    core = place[0]
    x_own = jnp.zeros(own.shape, F32)
    x_other = jnp.zeros(own.shape, F32)
    for k, piece in enumerate(pieces):
        chip = place[1 + k]
        value = piece[...]
        x_own += dot(window[:, pl.ds(pl.multiple_of((2 * chip + core) * n, n), n)], value)
        x_other += dot(swapped[:, pl.ds(pl.multiple_of(chip * n, n), n)], value)
    own[...] = x_own
    other[...] = x_other
    (a, b), (c, d) = halves(x_own), halves(x_other)
    total[...] = (dot_t(mine[...], a) + dot_t(sibling[...], c)) + (dot_t(mine[...], b) + dot_t(sibling[...], d))


def column_one_body(place, own, received, w_one, m_two, cross, column, carried, keep, send):
    exact = -(w_one[...].astype(F32) * (own[...] + received[...]))
    rounded = exact.astype(BF16)
    column[...] = rounded
    carried[...] = dot(rounded, cross[...])
    both = dot_t(m_two[...], rounded)
    half = both.shape[0] // 2
    first = place[0] == 0
    keep[...] = jnp.where(first, both[:half], both[half:])
    send[...] = jnp.where(first, both[half:], both[:half])


def column_two_body(own, received, w_two, carried, column):
    image = own[...] + received[...]
    column[...] = (-(w_two[...].astype(F32) * (image + carried[...]))).astype(BF16)


def pack_body(place, one, two, keep, send):
    n = one.shape[0]
    half = n // 2
    row = lax.broadcasted_iota(jnp.int32, (n, n), 0)
    col = lax.broadcasted_iota(jnp.int32, (n, n), 1)
    second = two[...]
    both = jnp.where(row <= col, one[...], second)
    diagonal = jnp.sum(jnp.where(row == col, second, 0.0), axis=0, keepdims=True)
    diagonal = jnp.broadcast_to(diagonal, (keep.shape[0] - half, n))
    first = place[0] == 0
    keep[:half] = jnp.where(first, both[:half], both[half:])
    send[:half] = jnp.where(first, both[half:], both[:half])
    keep[half:] = diagonal
    send[half:] = diagonal


def last_body(place, pack_a, pack_b, cross_a, cross_b, cross, diag_one, diag_two, block_one, edge, block_two):
    n = cross.shape[0]
    half = n // 2
    first = place[0] == 0

    def whole(a, b):
        return jnp.concatenate([jnp.where(first, a, b), jnp.where(first, b, a)], axis=0)

    row = lax.broadcasted_iota(jnp.int32, (n, n), 0)
    col = lax.broadcasted_iota(jnp.int32, (n, n), 1)
    packed = whole(pack_a[:half], pack_b[:half])
    turned = packed.T
    diagonal = jnp.where(first, pack_a[half : half + 1], pack_b[half : half + 1])
    s_one = jnp.where(row <= col, packed, turned)
    s_two = jnp.where(row > col, packed, turned)
    s_two = jnp.where(row == col, jnp.broadcast_to(diagonal, (n, n)), s_two)
    cross_sum = whole(cross_a[...], cross_b[...])
    c = cross[...]
    one = diag_one[...] + s_one
    block_one[...] = one
    a, b = halves(one)
    out = -(cross_sum.T + (dot(a, c) + dot(b, c)))
    edge[...] = out
    a, b = halves(out)
    d, e = halves(cross_sum)
    block_two[...] = diag_two[...] + s_two + (dot(d, c) + dot(e, c)) - (dot_t(c, a) + dot_t(c, b))


def local(
    inverse_window, panel_one, panel_two, cross_block, diag_one, diag_two, row_super, struct_mask, *, size
):
    chips = size // 2
    rows, width = panel_one.shape
    half = width // 2
    ring = [2 * r if r < chips // 2 else 2 * (chips - 1 - r) + 1 for r in range(chips)]
    position = [ring.index(t) for t in range(chips)]
    ahead = [(2 * ring[r] + c, 2 * ring[(r + 1) % chips] + c) for r in range(chips) for c in (0, 1)]
    back = [(b, a) for a, b in ahead]
    flip = [[(i, i ^ (1 << b)) for i in range(size)] for b in range(size.bit_length() - 1)]

    def send(x, perm):
        return lax.ppermute(x, AXIS, perm)

    me = lax.axis_index(AXIS)
    core = me % 2
    spot = jnp.array(position, jnp.int32)[me // 2]

    def chip_at(offset):
        return jnp.array(ring, jnp.int32)[(spot + offset + chips) % chips]

    where = core.reshape(1).astype(jnp.int32)

    square = ((rows, width), F32)
    tile = ((rows, width), BF16)
    m_one, m_two, w_one, w_two = call(
        mask_body,
        "mask",
        (tile, tile, tile, tile),
        (struct_mask, row_super.reshape(1, -1), panel_one, panel_two),
        n_smem=1,
    )
    (window_part,) = call(
        swap_body, "swap", (((rows, inverse_window.shape[1] // 2), BF16),), (where, inverse_window), n_smem=1
    )

    steps = chips // 2
    one, two, order_one, order_two = [m_one], [m_two], [0], [0]
    one_up = one_down = m_one
    two_up = two_down = m_two
    for k in range(1, steps):
        one_up, one_down = send(one_up, ahead), send(one_down, back)
        two_up, two_down = send(two_up, ahead), send(two_down, back)
        one += [one_up, one_down]
        two += [two_up, two_down]
        order_one += [-k, k]
        order_two += [-k, k]
    one.append(send(one_up, ahead))
    two.append(send(two_down, back))
    order_one.append(-steps)
    order_two.append(steps)

    swapped = send(window_part, flip[0])
    sibling_one = send(m_one, flip[0])
    sibling_two = send(m_two, flip[0])
    flops = 2 * 2 * rows * width * (width + inverse_window.shape[1] // 2)

    def image(name, order, pieces, mine, sibling):
        place = jnp.stack([core] + [chip_at(d) for d in order]).astype(jnp.int32)
        return call(
            image_body,
            name,
            (square, square, ((width, width), F32)),
            (place, inverse_window, swapped, mine, sibling, *pieces),
            n_smem=1,
            flops=flops,
        )

    own_one, other_one, total_one = image("image_one", order_one, one, m_one, sibling_one)
    received_one = send(other_one, flip[0])
    column_one, carried, keep_x, send_x = call(
        column_one_body,
        "column_one",
        (tile, square, ((half, width), F32), ((half, width), F32)),
        (where, own_one, received_one, w_one, m_two, cross_block),
        n_smem=1,
    )
    own_two, other_two, total_two = image("image_two", order_two, two, m_two, sibling_two)
    keep_p, send_p = call(
        pack_body,
        "pack",
        (((half + 16, width), F32), ((half + 16, width), F32)),
        (where, total_one, total_two),
        n_smem=1,
    )
    received_two = send(other_two, flip[0])
    (column_two,) = call(column_two_body, "column_two", (tile,), (own_two, received_two, w_two, carried))

    def summed(keep, away):
        value = keep + send(away, flip[0])
        for perm in flip[1:]:
            value = value.astype(BF16)
            value = value.astype(F32) + send(value, perm).astype(F32)
        return value, send(value, flip[0])

    cross_a, cross_b = summed(keep_x, send_x)
    pack_a, pack_b = summed(keep_p, send_p)
    full = ((width, width), F32)
    block_one, edge_block, block_two = call(
        last_body,
        "last",
        (full, full, full),
        (where, pack_a, pack_b, cross_a, cross_b, cross_block, diag_one, diag_two),
        n_smem=1,
    )
    return column_one, block_one, column_two, edge_block, block_two


def solution(mesh):
    return jax.shard_map(
        functools.partial(local, size=mesh.shape[AXIS]),
        mesh=mesh,
        in_specs=(
            P(("pole", "prow"), None),
            P(("pole", "prow"), None),
            P(("pole", "prow"), None),
            P("pole", None),
            P("pole", None),
            P("pole", None),
            P("prow"),
            P(),
        ),
        out_specs=(
            P(("pole", "prow"), None),
            P("pole", None),
            P(("pole", "prow"), None),
            P("pole", None),
            P("pole", None),
        ),
        check_vma=False,
    )
```

```python
import functools

import jax
import jax.numpy as jnp
from jax import lax
from jax.experimental import pallas as pl
from jax.experimental.pallas import tpu as pltpu
from jax.sharding import PartitionSpec as P

F32, BF16 = jnp.float32, jnp.bfloat16
AXIS = "prow"
VMEM = pl.BlockSpec(memory_space=pltpu.VMEM)
SMEM = pl.BlockSpec(memory_space=pltpu.SMEM)


def dot(left, right):
    return jnp.dot(left, right, preferred_element_type=F32)


def dot_t(left, right):
    return lax.dot_general(left, right, (((0,), (0,)), ((), ())), preferred_element_type=F32)


def halves(x):
    high = x.astype(BF16)
    return high, (x - high.astype(F32)).astype(BF16)


def call(body, name, outs, args, n_smem=0, flops=0, aliases=None):
    size = sum(a.size * a.dtype.itemsize for a in args)
    return pl.pallas_call(
        body,
        name=name,
        out_shape=tuple(jax.ShapeDtypeStruct(s, d) for s, d in outs),
        in_specs=[SMEM] * n_smem + [VMEM] * (len(args) - n_smem),
        out_specs=tuple(VMEM for _ in outs),
        input_output_aliases=aliases or {},
        compiler_params=pltpu.CompilerParams(vmem_limit_bytes=16 << 20),
        cost_estimate=pl.CostEstimate(flops=flops, bytes_accessed=size, transcendentals=0),
    )(*args)


def chip_of(position, chips):
    return jnp.where(position < chips // 2, 2 * position, 2 * (chips - 1 - position) + 1)


def chip_at(chip, offset, chips):
    position = jnp.where(chip % 2 == 0, chip // 2, chips - 1 - chip // 2)
    return chip_of((position + offset + chips) % chips, chips)


def mask_body(table, rows, one, two, m_one, m_two, w_one, w_two):
    n = one.shape[0]
    index = rows[...]
    on_diagonal = lax.broadcasted_iota(jnp.int32, (n, n), 0) == lax.broadcasted_iota(jnp.int32, (n, n), 1)
    ones = jnp.ones((n, n), BF16)
    for which, panel, masked, weights in ((0, one, m_one, w_one), (1, two, m_two, w_two)):
        weight = jnp.zeros(index.shape, F32)
        for s in range(table.shape[1]):
            weight = jnp.where(index == s, table[which, s].astype(F32), weight)
        chosen = jnp.where(on_diagonal, jnp.broadcast_to(weight, (n, n)), 0.0).astype(BF16)
        masked[...] = dot(chosen, panel[...]).astype(BF16)
        weights[...] = dot(chosen, ones).astype(BF16)


def swap_body(window, out):
    width = out.shape[0]
    other = 1 - lax.axis_index(AXIS) % 2
    for t in range(out.shape[1] // width):
        out[:, t * width : (t + 1) * width] = window[:, pl.ds(pl.multiple_of((2 * t + other) * width, width), width)]


def add_products(offsets, window, swapped, pieces, x_own, x_other):
    n = window.shape[0]
    me = lax.axis_index(AXIS)
    chip, core = me // 2, me % 2
    for offset, piece in zip(offsets, pieces, strict=True):
        t = chip_at(chip, offset, window.shape[1] // (2 * n))
        value = piece[...]
        x_own += dot(window[:, pl.ds(pl.multiple_of((2 * t + core) * n, n), n)], value)
        x_other += dot(swapped[:, pl.ds(pl.multiple_of(t * n, n), n)], value)
    return x_own, x_other


def image_first_body(offsets, window, swapped, *rest):
    pieces, (own, other) = rest[:-2], rest[-2:]
    zero = jnp.zeros(own.shape, F32)
    own[...], other[...] = add_products(offsets, window, swapped, pieces, zero, zero)


def image_more_body(offsets, window, swapped, own_in, other_in, *rest):
    pieces, (own, other) = rest[:-2], rest[-2:]
    own[...], other[...] = add_products(offsets, window, swapped, pieces, own_in[...], other_in[...])


def image_last_body(offsets, window, swapped, own_in, other_in, mine, sibling, *rest):
    pieces, (own, other, total) = rest[:-3], rest[-3:]
    x_own, x_other = add_products(offsets, window, swapped, pieces, own_in[...], other_in[...])
    own[...] = x_own
    other[...] = x_other
    (a, b), (c, d) = halves(x_own), halves(x_other)
    total[...] = (dot_t(mine[...], a) + dot_t(sibling[...], c)) + (dot_t(mine[...], b) + dot_t(sibling[...], d))


def column_one_body(own, received, w_one, m_two, cross, column, carried, keep, send):
    exact = -(w_one[...].astype(F32) * (own[...] + received[...]))
    rounded = exact.astype(BF16)
    column[...] = rounded
    carried[...] = dot(rounded, cross[...])
    both = dot_t(m_two[...], rounded)
    half = both.shape[0] // 2
    first = lax.axis_index(AXIS) % 2 == 0
    keep[...] = jnp.where(first, both[:half], both[half:])
    send[...] = jnp.where(first, both[half:], both[:half])


def column_two_body(own, received, w_two, carried, column):
    image = own[...] + received[...]
    column[...] = (-(w_two[...].astype(F32) * (image + carried[...]))).astype(BF16)


def pack_body(one, two, keep, send):
    n = one.shape[0]
    half = n // 2
    row = lax.broadcasted_iota(jnp.int32, (n, n), 0)
    col = lax.broadcasted_iota(jnp.int32, (n, n), 1)
    second = two[...]
    both = jnp.where(row <= col, one[...], second)
    diagonal = jnp.sum(jnp.where(row == col, second, 0.0), axis=0, keepdims=True)
    diagonal = jnp.broadcast_to(diagonal, (keep.shape[0] - half, n))
    first = lax.axis_index(AXIS) % 2 == 0
    keep[:half] = jnp.where(first, both[:half], both[half:])
    send[:half] = jnp.where(first, both[half:], both[:half])
    keep[half:] = diagonal
    send[half:] = diagonal


def last_body(pack_a, pack_b, cross_a, cross_b, cross, diag_one, diag_two, block_one, edge, block_two):
    n = cross.shape[0]
    half = n // 2
    first = lax.axis_index(AXIS) % 2 == 0

    def whole(a, b):
        return jnp.concatenate([jnp.where(first, a, b), jnp.where(first, b, a)], axis=0)

    row = lax.broadcasted_iota(jnp.int32, (n, n), 0)
    col = lax.broadcasted_iota(jnp.int32, (n, n), 1)
    packed = whole(pack_a[:half], pack_b[:half])
    turned = packed.T
    diagonal = jnp.where(first, pack_a[half : half + 1], pack_b[half : half + 1])
    s_one = jnp.where(row <= col, packed, turned)
    s_two = jnp.where(row > col, packed, turned)
    s_two = jnp.where(row == col, jnp.broadcast_to(diagonal, (n, n)), s_two)
    cross_sum = whole(cross_a[...], cross_b[...])
    c = cross[...]
    one = diag_one[...] + s_one
    block_one[...] = one
    a, b = halves(one)
    out = -(cross_sum.T + (dot(a, c) + dot(b, c)))
    edge[...] = out
    a, b = halves(out)
    d, e = halves(cross_sum)
    block_two[...] = diag_two[...] + s_two + (dot(d, c) + dot(e, c)) - (dot_t(c, a) + dot_t(c, b))


def local(
    inverse_window, panel_one, panel_two, cross_block, diag_one, diag_two, row_super, struct_mask, *, size
):
    chips = size // 2
    rows, width = panel_one.shape
    half = width // 2
    ring = [2 * r if r < chips // 2 else 2 * (chips - 1 - r) + 1 for r in range(chips)]
    position = [ring.index(t) for t in range(chips)]
    ahead = [(2 * ring[r] + c, 2 * ring[(r + 1) % chips] + c) for r in range(chips) for c in (0, 1)]
    back = [(b, a) for a, b in ahead]
    flip = [[(i, i ^ (1 << b)) for i in range(size)] for b in range(size.bit_length() - 1)]

    def send(x, perm):
        return lax.ppermute(x, AXIS, perm)

    square = ((rows, width), F32)
    tile = ((rows, width), BF16)
    m_one, m_two, w_one, w_two = call(
        mask_body,
        "mask",
        (tile, tile, tile, tile),
        (struct_mask, row_super.reshape(1, -1), panel_one, panel_two),
        n_smem=1,
    )
    steps = chips // 2
    one, two = [(0, m_one)], [(0, m_two)]
    one_up = one_down = m_one
    two_up = two_down = m_two
    for k in range(1, steps):
        one_up, one_down = send(one_up, ahead), send(one_down, back)
        two_up, two_down = send(two_up, ahead), send(two_down, back)
        one += [(-k, one_up), (k, one_down)]
        two += [(-k, two_up), (k, two_down)]
    one.append((-steps, send(one_up, ahead)))
    two.append((steps, send(two_down, back)))

    window, _ = lax.optimization_barrier((inverse_window, one[1][1]))
    (window_part,) = call(swap_body, "swap", (((rows, inverse_window.shape[1] // 2), BF16),), (window,))
    swapped = send(window_part, flip[0])
    sibling_one = send(m_one, flip[0])
    sibling_two = send(m_two, flip[0])

    def image(name, pieces, mine, sibling):
        def stage(body, label, chosen, outs, *more, aliases=None):
            offsets, values = zip(*chosen, strict=True)
            return call(
                functools.partial(body, offsets),
                name + label,
                outs,
                (inverse_window, swapped, *more, *values),
                flops=2 * 2 * rows * width * width * len(chosen),
                aliases=aliases,
            )

        kept = {2: 0, 3: 1}
        own, other = stage(image_first_body, "_first", pieces[:3], (square, square))
        middle = pieces[3:-1]
        for i in range(0, len(middle), 4):
            own, other = stage(image_more_body, "_more", middle[i : i + 4], (square, square), own, other, aliases=kept)
        return stage(
            image_last_body, "_last", pieces[-1:], (square, square, ((width, width), F32)), own, other, mine, sibling, aliases=kept
        )

    own_one, other_one, total_one = image("image_one", one, m_one, sibling_one)
    received_one = send(other_one, flip[0])
    column_one, carried, keep_x, send_x = call(
        column_one_body,
        "column_one",
        (tile, square, ((half, width), F32), ((half, width), F32)),
        (own_one, received_one, w_one, m_two, cross_block),
    )
    own_two, other_two, total_two = image("image_two", two, m_two, sibling_two)
    keep_p, send_p = call(
        pack_body,
        "pack",
        (((half + 16, width), F32), ((half + 16, width), F32)),
        (total_one, total_two),
    )
    received_two = send(other_two, flip[0])
    (column_two,) = call(column_two_body, "column_two", (tile,), (own_two, received_two, w_two, carried))

    def summed(keep, away):
        value = keep + send(away, flip[0])
        for perm in flip[1:]:
            value = value.astype(BF16)
            value = value.astype(F32) + send(value, perm).astype(F32)
        return value, send(value, flip[0])

    cross_a, cross_b = summed(keep_x, send_x)
    pack_a, pack_b = summed(keep_p, send_p)
    full = ((width, width), F32)
    block_one, edge_block, block_two = call(
        last_body,
        "last",
        (full, full, full),
        (pack_a, pack_b, cross_a, cross_b, cross_block, diag_one, diag_two),
    )
    return column_one, block_one, column_two, edge_block, block_two


def solution(mesh):
    return jax.shard_map(
        functools.partial(local, size=mesh.shape[AXIS]),
        mesh=mesh,
        in_specs=(
            P(("pole", "prow"), None),
            P(("pole", "prow"), None),
            P(("pole", "prow"), None),
            P("pole", None),
            P("pole", None),
            P("pole", None),
            P("prow"),
            P(),
        ),
        out_specs=(
            P(("pole", "prow"), None),
            P("pole", None),
            P(("pole", "prow"), None),
            P("pole", None),
            P("pole", None),
        ),
        check_vma=False,
    )
```

```python
import functools

import jax
import jax.numpy as jnp
from jax import lax
from jax.experimental import pallas as pl
from jax.experimental.pallas import tpu as pltpu
from jax.sharding import PartitionSpec as P

F32, BF16 = jnp.float32, jnp.bfloat16
AXIS = "prow"
VMEM = pl.BlockSpec(memory_space=pltpu.VMEM)
SMEM = pl.BlockSpec(memory_space=pltpu.SMEM)
HBM = pl.BlockSpec(memory_space=pltpu.HBM)


def dot(left, right):
    return jnp.dot(left, right, preferred_element_type=F32)


def dot_t(left, right):
    return lax.dot_general(left, right, (((0,), (0,)), ((), ())), preferred_element_type=F32)


def halves(x):
    high = x.astype(BF16)
    return high, (x - high.astype(F32)).astype(BF16)


def call(body, name, outs, args, n_smem=0, flops=0, aliases=None, specs=None, scratch=()):
    size = sum(a.size * a.dtype.itemsize for a in args)
    return pl.pallas_call(
        body,
        name=name,
        out_shape=tuple(jax.ShapeDtypeStruct(s, d) for s, d in outs),
        in_specs=specs or [SMEM] * n_smem + [VMEM] * (len(args) - n_smem),
        out_specs=tuple(VMEM for _ in outs),
        input_output_aliases=aliases or {},
        scratch_shapes=scratch,
        compiler_params=pltpu.CompilerParams(vmem_limit_bytes=16 << 20),
        cost_estimate=pl.CostEstimate(flops=flops, bytes_accessed=size, transcendentals=0),
    )(*args)


def chip_of(position, chips):
    return jnp.where(position < chips // 2, 2 * position, 2 * (chips - 1 - position) + 1)


def chip_at(chip, offset, chips):
    position = jnp.where(chip % 2 == 0, chip // 2, chips - 1 - chip // 2)
    return chip_of((position + offset + chips) % chips, chips)


def in_hbm(x):
    return pltpu.with_memory_space_constraint(x, pltpu.HBM)


def diagonal_of(weight):
    n = weight.shape[1]
    on = lax.broadcasted_iota(jnp.int32, (n, n), 0) == lax.broadcasted_iota(jnp.int32, (n, n), 1)
    return jnp.where(on, jnp.broadcast_to(weight, (n, n)), 0.0).astype(BF16)


def mask_body(table, rows, one, two, window, m_one, m_two, weights, window_v, table_v, rows_v, one_v, two_v, sems):
    moves = (table, table_v), (rows, rows_v), (one, one_v), (two, two_v), (window, window_v)
    copies = [pltpu.make_async_copy(src, dst, sems.at[i]) for i, (src, dst) in enumerate(moves)]
    for copy in copies:
        copy.start()
    copies[0].wait()
    copies[1].wait()
    index = rows_v[...]
    for which, panel, masked in ((0, one_v, m_one), (1, two_v, m_two)):
        weight = jnp.zeros(index.shape, F32)
        for s in range(table.shape[1]):
            weight = jnp.where(index == s, table_v[which, s].astype(F32), weight)
        weights[which : which + 1] = weight
        chosen = diagonal_of(weight)
        copies[2 + which].wait()
        masked[...] = dot(chosen, panel[...]).astype(BF16)
    copies[4].wait()


def add_products(offsets, window, swapped, pieces, x_own, x_other):
    n = window.shape[0]
    me = lax.axis_index(AXIS)
    for offset, piece in zip(offsets, pieces, strict=True):
        block = 2 * chip_at(me // 2, offset, window.shape[1] // (2 * n)) + me % 2
        columns = pl.ds(pl.multiple_of(block * n, n), n)
        value = piece[...]
        x_own += dot(window[:, columns], value)
        x_other += dot(swapped[:, columns], value)
    return x_own, x_other


def image_first_body(offsets, window, swapped, *rest):
    pieces, (own, other) = rest[:-2], rest[-2:]
    zero = jnp.zeros(own.shape, F32)
    own[...], other[...] = add_products(offsets, window, swapped, pieces, zero, zero)


def image_more_body(offsets, window, swapped, own_in, other_in, *rest):
    pieces, (own, other) = rest[:-2], rest[-2:]
    own[...], other[...] = add_products(offsets, window, swapped, pieces, own_in[...], other_in[...])


def image_last_body(offsets, window, swapped, own_in, other_in, mine, sibling, *rest):
    pieces, (own, other, total) = rest[:-3], rest[-3:]
    x_own, x_other = add_products(offsets, window, swapped, pieces, own_in[...], other_in[...])
    own[...] = x_own
    other[...] = x_other
    (a, b), (c, d) = halves(x_own), halves(x_other)
    total[...] = (dot_t(mine[...], a) + dot_t(sibling[...], c)) + (dot_t(mine[...], b) + dot_t(sibling[...], d))


def column_one_body(own, received, weights, m_two, cross, column, carried, keep, send):
    n = column.shape[0]
    weight = dot(diagonal_of(weights[0:1]), jnp.ones((n, n), BF16))
    exact = -(weight * (own[...] + received[...]))
    rounded = exact.astype(BF16)
    column[...] = rounded
    carried[...] = dot(rounded, cross[...])
    both = dot_t(m_two[...], rounded)
    half = both.shape[0] // 2
    first = lax.axis_index(AXIS) % 2 == 0
    keep[...] = jnp.where(first, both[:half], both[half:])
    send[...] = jnp.where(first, both[half:], both[:half])


def column_two_body(own, received, weights, carried, column):
    n = column.shape[0]
    weight = dot(diagonal_of(weights[1:2]), jnp.ones((n, n), BF16))
    image = own[...] + received[...]
    column[...] = (-(weight * (image + carried[...]))).astype(BF16)


def pack_body(one, two, keep, send):
    n = one.shape[0]
    half = n // 2
    row = lax.broadcasted_iota(jnp.int32, (n, n), 0)
    col = lax.broadcasted_iota(jnp.int32, (n, n), 1)
    second = two[...]
    both = jnp.where(row <= col, one[...], second)
    diagonal = jnp.sum(jnp.where(row == col, second, 0.0), axis=0, keepdims=True)
    diagonal = jnp.broadcast_to(diagonal, (keep.shape[0] - half, n))
    first = lax.axis_index(AXIS) % 2 == 0
    keep[:half] = jnp.where(first, both[:half], both[half:])
    send[:half] = jnp.where(first, both[half:], both[:half])
    keep[half:] = diagonal
    send[half:] = diagonal


def last_body(pack_a, pack_b, cross_a, cross_b, cross, diag_one, diag_two, block_one, edge, block_two):
    n = cross.shape[0]
    half = n // 2
    first = lax.axis_index(AXIS) % 2 == 0

    def whole(a, b):
        return jnp.concatenate([jnp.where(first, a, b), jnp.where(first, b, a)], axis=0)

    row = lax.broadcasted_iota(jnp.int32, (n, n), 0)
    col = lax.broadcasted_iota(jnp.int32, (n, n), 1)
    packed = whole(pack_a[:half], pack_b[:half])
    turned = packed.T
    diagonal = jnp.where(first, pack_a[half : half + 1], pack_b[half : half + 1])
    s_one = jnp.where(row <= col, packed, turned)
    s_two = jnp.where(row > col, packed, turned)
    s_two = jnp.where(row == col, jnp.broadcast_to(diagonal, (n, n)), s_two)
    cross_sum = whole(cross_a[...], cross_b[...])
    c = cross[...]
    one = diag_one[...] + s_one
    block_one[...] = one
    a, b = halves(one)
    out = -(cross_sum.T + (dot(a, c) + dot(b, c)))
    edge[...] = out
    a, b = halves(out)
    d, e = halves(cross_sum)
    block_two[...] = diag_two[...] + s_two + (dot(d, c) + dot(e, c)) - (dot_t(c, a) + dot_t(c, b))


def local(
    inverse_window, panel_one, panel_two, cross_block, diag_one, diag_two, row_super, struct_mask, *, size
):
    chips = size // 2
    rows, width = panel_one.shape
    half = width // 2
    ring = [2 * r if r < chips // 2 else 2 * (chips - 1 - r) + 1 for r in range(chips)]
    position = [ring.index(t) for t in range(chips)]
    ahead = [(2 * ring[r] + c, 2 * ring[(r + 1) % chips] + c) for r in range(chips) for c in (0, 1)]
    back = [(b, a) for a, b in ahead]
    flip = [[(i, i ^ (1 << b)) for i in range(size)] for b in range(size.bit_length() - 1)]

    def send(x, perm):
        return lax.ppermute(x, AXIS, perm)

    square = ((rows, width), F32)
    tile = ((rows, width), BF16)
    m_one, m_two, weights, window = call(
        mask_body,
        "mask",
        (tile, tile, ((2, rows), F32), (inverse_window.shape, BF16)),
        tuple(map(in_hbm, (struct_mask, row_super.reshape(1, -1), panel_one, panel_two, inverse_window))),
        specs=[HBM] * 5,
        scratch=[
            pltpu.SMEM(struct_mask.shape, jnp.int32),
            pltpu.VMEM((1, rows), jnp.int32),
            pltpu.VMEM((rows, width), BF16),
            pltpu.VMEM((rows, width), BF16),
            pltpu.SemaphoreType.DMA((5,)),
        ],
    )

    steps = chips // 2
    one, two = [(0, m_one)], [(0, m_two)]
    one_up = one_down = m_one
    two_up = two_down = m_two
    for k in range(1, steps):
        one_up, one_down = send(one_up, ahead), send(one_down, back)
        two_up, two_down = send(two_up, ahead), send(two_down, back)
        one += [(-k, one_up), (k, one_down)]
        two += [(-k, two_up), (k, two_down)]
    one.append((-steps, send(one_up, ahead)))
    two.append((steps, send(two_down, back)))
    after = one[-3][1], one[-2][1], two[-2][1], two[-3][1]

    swapped = send(window, flip[0])
    sibling_one = send(m_one, flip[0])
    sibling_two = send(m_two, flip[0])

    def stage(body, name, chosen, outs, *more, aliases=None):
        offsets, values = zip(*chosen, strict=True)
        return call(
            functools.partial(body, offsets),
            name,
            outs,
            (window, swapped, *more, *values),
            flops=2 * 2 * rows * width * width * len(chosen),
            aliases=aliases,
        )

    def begin(name, pieces, after):
        pieces = [(offset, lax.optimization_barrier((piece, after))[0]) for offset, piece in pieces]
        own, other = stage(image_first_body, name + "_first", pieces[:3], (square, square))
        for i in range(3, len(pieces), 4):
            own, other = stage(
                image_more_body, name + "_more", pieces[i : i + 4], (square, square), own, other, aliases={2: 0, 3: 1}
            )
        return own, other

    def finish(name, last, own, other, panel, sibling):
        outs = square, square, ((width, width), F32)
        return stage(image_last_body, name, [last], outs, own, other, panel, sibling, aliases={2: 0, 3: 1})

    def half_sum(keep, away):
        return keep + send(away, flip[0])

    own_one, other_one, total_one = finish("image_one", one[-1], *begin("image_one", one[:-1], after), m_one, sibling_one)
    received_one = send(other_one, flip[0])
    column_one, carried, keep_x, send_x = call(
        column_one_body,
        "column_one",
        (tile, square, ((half, width), F32), ((half, width), F32)),
        (own_one, received_one, weights, m_two, cross_block),
    )
    cross_half = half_sum(keep_x, send_x)
    own_two, other_two = begin("image_two", two[:-1], after)
    own_two, other_two, total_two = finish("image_two", two[-1], own_two, other_two, m_two, sibling_two)
    keep_p, send_p = call(
        pack_body, "pack", (((half + 16, width), F32), ((half + 16, width), F32)), (total_one, total_two)
    )
    received_two = send(other_two, flip[0])
    (column_two,) = call(column_two_body, "column_two", (tile,), (own_two, received_two, weights, carried))

    def summed(value):
        for perm in flip[1:]:
            value = value.astype(BF16)
            value = value.astype(F32) + send(value, perm).astype(F32)
        return value, send(value, flip[0])

    cross_a, cross_b = summed(cross_half)
    pack_a, pack_b = summed(half_sum(keep_p, send_p))
    full = ((width, width), F32)
    block_one, edge_block, block_two = call(
        last_body,
        "last",
        (full, full, full),
        (pack_a, pack_b, cross_a, cross_b, cross_block, diag_one, diag_two),
    )
    return column_one, block_one, column_two, edge_block, block_two


def solution(mesh):
    return jax.shard_map(
        functools.partial(local, size=mesh.shape[AXIS]),
        mesh=mesh,
        in_specs=(
            P(("pole", "prow"), None),
            P(("pole", "prow"), None),
            P(("pole", "prow"), None),
            P("pole", None),
            P("pole", None),
            P("pole", None),
            P("prow"),
            P(),
        ),
        out_specs=(
            P(("pole", "prow"), None),
            P("pole", None),
            P(("pole", "prow"), None),
            P("pole", None),
            P("pole", None),
        ),
        check_vma=False,
    )
```

```python
import functools

import jax
import jax.numpy as jnp
from jax import lax
from jax.experimental import pallas as pl
from jax.experimental.pallas import tpu as pltpu
from jax.sharding import PartitionSpec as P

F32, BF16 = jnp.float32, jnp.bfloat16
AXIS = "prow"
VMEM = pl.BlockSpec(memory_space=pltpu.VMEM)
SMEM = pl.BlockSpec(memory_space=pltpu.SMEM)
HBM = pl.BlockSpec(memory_space=pltpu.HBM)


def dot(left, right):
    return jnp.dot(left, right, preferred_element_type=F32)


def dot_t(left, right):
    return lax.dot_general(left, right, (((0,), (0,)), ((), ())), preferred_element_type=F32)


def halves(x):
    high = x.astype(BF16)
    return high, (x - high.astype(F32)).astype(BF16)


def call(body, name, outs, args, n_smem=0, flops=0, aliases=None, specs=None, scratch=()):
    size = sum(a.size * a.dtype.itemsize for a in args)
    return pl.pallas_call(
        body,
        name=name,
        out_shape=tuple(jax.ShapeDtypeStruct(s, d) for s, d in outs),
        in_specs=specs or [SMEM] * n_smem + [VMEM] * (len(args) - n_smem),
        out_specs=tuple(VMEM for _ in outs),
        input_output_aliases=aliases or {},
        scratch_shapes=scratch,
        compiler_params=pltpu.CompilerParams(vmem_limit_bytes=16 << 20),
        cost_estimate=pl.CostEstimate(flops=flops, bytes_accessed=size, transcendentals=0),
    )(*args)


def chip_of(position, chips):
    return jnp.where(position < chips // 2, 2 * position, 2 * (chips - 1 - position) + 1)


def chip_at(chip, offset, chips):
    position = jnp.where(chip % 2 == 0, chip // 2, chips - 1 - chip // 2)
    return chip_of((position + offset + chips) % chips, chips)


def in_hbm(x):
    return pltpu.with_memory_space_constraint(x, pltpu.HBM)


def diagonal_of(weight):
    n = weight.shape[1]
    on = lax.broadcasted_iota(jnp.int32, (n, n), 0) == lax.broadcasted_iota(jnp.int32, (n, n), 1)
    return jnp.where(on, jnp.broadcast_to(weight, (n, n)), 0.0).astype(BF16)


def mask_body(table, rows, one, two, window, m_one, m_two, stack, weights, window_v, table_v, rows_v, one_v, two_v, sems):
    moves = (table, table_v), (rows, rows_v), (one, one_v), (two, two_v), (window, window_v)
    copies = [pltpu.make_async_copy(src, dst, sems.at[i]) for i, (src, dst) in enumerate(moves)]
    for copy in copies:
        copy.start()
    copies[0].wait()
    copies[1].wait()
    index = rows_v[...]
    n = one.shape[0]
    for which, panel, masked in ((0, one_v, m_one), (1, two_v, m_two)):
        weight = jnp.zeros(index.shape, F32)
        for s in range(table.shape[1]):
            weight = jnp.where(index == s, table_v[which, s].astype(F32), weight)
        weights[which : which + 1] = weight
        chosen = diagonal_of(weight)
        copies[2 + which].wait()
        value = dot(chosen, panel[...]).astype(BF16)
        masked[...] = value
        stack[which * n : (which + 1) * n] = value
    stack[2 * n :] = dot(diagonal_of(weights[0:1]), m_two[...]).astype(BF16)
    copies[4].wait()


def product(offset, window, swapped, piece):
    n = window.shape[0]
    me = lax.axis_index(AXIS)
    block = 2 * chip_at(me // 2, offset, window.shape[1] // (2 * n)) + me % 2
    columns = pl.ds(pl.multiple_of(block * n, n), n)
    value = piece[...]
    return dot(window[:, columns], value), dot(swapped[:, columns], value)


def plus(left, right, scale=1.0):
    return tuple(a + scale * b for a, b in zip(left, right, strict=True))


def add_products(total, chosen, window, swapped):
    for offset, piece in chosen:
        total = plus(total, product(offset, window, swapped, piece))
    return total


def early_body(window, swapped, one, up, down, two, back, *outs):
    zero = (jnp.zeros(one.shape, F32),) * 2
    own = product(0, window, swapped, one)
    side = plus(add_products(zero, up, window, swapped), own, 0.5)
    whole = plus(add_products(side, down, window, swapped), own, 0.5)
    own = product(0, window, swapped, two)
    side_two = plus(add_products(zero, back, window, swapped), own, 0.5)
    whole_two = plus(side_two, own, 0.5)
    for out, value in zip(outs, (*side, *whole, *side_two, *whole_two), strict=True):
        out[...] = value


def gram(stack, sibling, which, images):
    (a, b), (c, d) = halves(images[0]), halves(images[1])
    n = images[0].shape[0]
    mine, sibling = (x[which * n : (which + 1) * n] for x in (stack, sibling))
    return (dot_t(mine, a) + dot_t(sibling, c)) + (dot_t(mine, b) + dot_t(sibling, d))


def late_body(steps, window, swapped, *rest):
    sums, (stack, sibling, one, two), outs, (keep, send) = rest[:8], rest[8:12], rest[12:16], rest[16:]
    sums = [(sums[i][...], sums[i + 1][...]) for i in range(0, 8, 2)]
    far = product(-steps, window, swapped, one)
    image_one = plus(sums[1], far)
    first = gram(stack, sibling, 0, plus(sums[0], far, 0.5))
    far = product(steps, window, swapped, two)
    image_two = plus(sums[3], far)
    second = gram(stack, sibling, 1, plus(sums[2], far, 0.5))
    cross = -gram(stack, sibling, 2, image_one)
    for out, value in zip(outs, (*image_one, *image_two), strict=True):
        out[...] = value

    n = first.shape[0]
    half = n // 2
    row = lax.broadcasted_iota(jnp.int32, (n, n), 0)
    col = lax.broadcasted_iota(jnp.int32, (n, n), 1)
    second = second + second.T
    both = jnp.where(row <= col, first + first.T, second)
    diagonal = jnp.sum(jnp.where(row == col, second, 0.0), axis=0, keepdims=True)
    diagonal = jnp.broadcast_to(diagonal, (keep.shape[0] - n, n))
    low = lax.axis_index(AXIS) % 2 == 0
    for out, mine in ((keep, low), (send, jnp.logical_not(low))):
        out[:half] = jnp.where(mine, both[:half], both[half:])
        out[half:-half] = diagonal
        out[-half:] = jnp.where(mine, cross[:half], cross[half:])


def rest_body(window, swapped, own_in, other_in, up, own, other):
    own[...], other[...] = add_products((own_in[...], other_in[...]), up, window, swapped)


def row_weights(weights, which):
    n = weights.shape[1]
    return dot(diagonal_of(weights[which : which + 1]), jnp.ones((n, n), BF16))


def columns_body(own_one, received_one, own_two, received_two, weights, cross, column_one, column_two):
    rounded = (-(row_weights(weights, 0) * (own_one[...] + received_one[...]))).astype(BF16)
    column_one[...] = rounded
    image = own_two[...] + received_two[...]
    column_two[...] = (-(row_weights(weights, 1) * (image + dot(rounded, cross[...])))).astype(BF16)


def last_body(pack_a, pack_b, cross_a, cross_b, cross, diag_one, diag_two, block_one, edge, block_two):
    n = cross.shape[0]
    half = n // 2
    first = lax.axis_index(AXIS) % 2 == 0

    def whole(a, b):
        return jnp.concatenate([jnp.where(first, a, b), jnp.where(first, b, a)], axis=0)

    row = lax.broadcasted_iota(jnp.int32, (n, n), 0)
    col = lax.broadcasted_iota(jnp.int32, (n, n), 1)
    packed = whole(pack_a[:half], pack_b[:half])
    turned = packed.T
    diagonal = jnp.where(first, pack_a[half : half + 1], pack_b[half : half + 1])
    s_one = jnp.where(row <= col, packed, turned)
    s_two = jnp.where(row > col, packed, turned)
    s_two = jnp.where(row == col, jnp.broadcast_to(diagonal, (n, n)), s_two)
    cross_sum = whole(cross_a[...], cross_b[...])
    c = cross[...]
    one = diag_one[...] + s_one
    block_one[...] = one
    a, b = halves(one)
    out = -(cross_sum.T + (dot(a, c) + dot(b, c)))
    edge[...] = out
    a, b = halves(out)
    d, e = halves(cross_sum)
    block_two[...] = diag_two[...] + s_two + (dot(d, c) + dot(e, c)) - (dot_t(c, a) + dot_t(c, b))


def local(
    inverse_window, panel_one, panel_two, cross_block, diag_one, diag_two, row_super, struct_mask, *, size
):
    chips = size // 2
    rows, width = panel_one.shape
    half = width // 2
    ring = [2 * r if r < chips // 2 else 2 * (chips - 1 - r) + 1 for r in range(chips)]
    ahead = [(2 * ring[r] + c, 2 * ring[(r + 1) % chips] + c) for r in range(chips) for c in (0, 1)]
    back = [(b, a) for a, b in ahead]
    flip = [[(i, i ^ (1 << b)) for i in range(size)] for b in range(size.bit_length() - 1)]

    def send(x, perm):
        return lax.ppermute(x, AXIS, perm)

    square = ((rows, width), F32)
    tile = ((rows, width), BF16)
    m_one, m_two, stack, weights, window = call(
        mask_body,
        "mask",
        (tile, tile, ((3 * rows, width), BF16), ((2, rows), F32), (inverse_window.shape, BF16)),
        tuple(map(in_hbm, (struct_mask, row_super.reshape(1, -1), panel_one, panel_two, inverse_window))),
        specs=[HBM] * 5,
        scratch=[
            pltpu.SMEM(struct_mask.shape, jnp.int32),
            pltpu.VMEM((1, rows), jnp.int32),
            pltpu.VMEM((rows, width), BF16),
            pltpu.VMEM((rows, width), BF16),
            pltpu.SemaphoreType.DMA((5,)),
        ],
    )

    steps = chips // 2
    one_up, one_down, two_up, two_down = [m_one], [m_one], [m_two], [m_two]
    for k in range(1, steps):
        one_up.append(send(one_up[-1], ahead))
        two_down.append(send(two_down[-1], back))
        one_down.append(send(one_down[-1], back))
        if k < steps - 1:
            two_up.append(send(two_up[-1], ahead))
    one_far = send(one_up[-1], ahead)
    two_far = send(two_down[-1], back)
    swapped = send(window, flip[0])
    sibling = send(stack, flip[0])

    def early_refs(*refs):
        inputs, outs = refs[: len(early_in)], refs[len(early_in) :]
        fixed, pieces = inputs[:2], inputs[2:]
        n = steps - 1
        one, up, down = pieces[0], pieces[1 : 1 + n], pieces[1 + n : 1 + 2 * n]
        two, behind = pieces[1 + 2 * n], pieces[2 + 2 * n :]
        early_body(
            *fixed,
            one,
            [(-k, p) for k, p in enumerate(up, 1)],
            [(k, p) for k, p in enumerate(down, 1)],
            two,
            [(k, p) for k, p in enumerate(behind, 1)],
            *outs,
        )

    one_up[-1], *_ = lax.optimization_barrier((one_up[-1], *two_up))
    early_in = (
        *(window, swapped),
        *one_up,
        *one_down[1:],
        *two_down,
    )
    block_flops = 4 * rows * width * width
    early = call(early_refs, "early", (square,) * 8, early_in, flops=block_flops * (3 * steps + 1))
    tall = ((width + 16, width), F32)
    own_one, other_one, own_two, other_two, keep, away = call(
        functools.partial(late_body, steps),
        "late",
        (square,) * 4 + (tall, tall),
        (window, swapped, *early, stack, sibling, one_far, two_far),
        flops=block_flops * 8,
    )
    value = keep + send(away, flip[0])
    value, last_up = lax.optimization_barrier((value, two_up[-1]))
    two_up.append(send(last_up, ahead))

    stages = []

    def summed(value):
        for perm in flip[1:]:
            value = value.astype(BF16)
            value = value.astype(F32) + send(value, perm).astype(F32)
            stages.append(value)
        return value

    pack_a = summed(value[:-half])
    cross_a = summed(value[-half:])
    pack_b, cross_b = send(pack_a, flip[0]), send(cross_a, flip[0])

    received_one = send(other_one, flip[0])
    def rest_refs(*refs):
        inputs, outs = refs[: len(rest_in)], refs[len(rest_in) :]
        rest_body(*inputs[:4], [(-k, p) for k, p in enumerate(inputs[4:], 1)], *outs)

    rest_in = (window, swapped, own_two, other_two, *two_up[1:])
    own_two, other_two = call(rest_refs, "rest", (square,) * 2, rest_in, flops=block_flops * (steps - 1))
    received_two = send(other_two, flip[0])
    column_one, column_two = call(
        columns_body,
        "columns",
        (tile, tile),
        (own_one, received_one, own_two, received_two, weights, cross_block),
    )
    pack_b, column_two = lax.optimization_barrier((pack_b, column_two))
    full = ((width, width), F32)
    block_one, edge_block, block_two = call(
        last_body,
        "last",
        (full, full, full),
        (pack_a, pack_b, cross_a, cross_b, cross_block, diag_one, diag_two),
    )
    return column_one, block_one, column_two, edge_block, block_two


def solution(mesh):
    return jax.shard_map(
        functools.partial(local, size=mesh.shape[AXIS]),
        mesh=mesh,
        in_specs=(
            P(("pole", "prow"), None),
            P(("pole", "prow"), None),
            P(("pole", "prow"), None),
            P("pole", None),
            P("pole", None),
            P("pole", None),
            P("prow"),
            P(),
        ),
        out_specs=(
            P(("pole", "prow"), None),
            P("pole", None),
            P(("pole", "prow"), None),
            P("pole", None),
            P("pole", None),
        ),
        check_vma=False,
    )
```

```python
import functools

import jax
import jax.numpy as jnp
from jax import lax
from jax.experimental import pallas as pl
from jax.experimental.pallas import tpu as pltpu
from jax.sharding import PartitionSpec as P

F32, BF16 = jnp.float32, jnp.bfloat16
AXIS = "prow"
VMEM = pl.BlockSpec(memory_space=pltpu.VMEM)
SMEM = pl.BlockSpec(memory_space=pltpu.SMEM)
HBM = pl.BlockSpec(memory_space=pltpu.HBM)


def dot(left, right):
    return jnp.dot(left, right, preferred_element_type=F32)


def dot_t(left, right):
    return lax.dot_general(left, right, (((0,), (0,)), ((), ())), preferred_element_type=F32)


def halves(x):
    high = x.astype(BF16)
    return high, (x - high.astype(F32)).astype(BF16)


def call(body, name, outs, args, n_smem=0, flops=0, aliases=None, specs=None, scratch=()):
    size = sum(a.size * a.dtype.itemsize for a in args)
    return pl.pallas_call(
        body,
        name=name,
        out_shape=tuple(jax.ShapeDtypeStruct(s, d) for s, d in outs),
        in_specs=specs or [SMEM] * n_smem + [VMEM] * (len(args) - n_smem),
        out_specs=tuple(VMEM for _ in outs),
        input_output_aliases=aliases or {},
        scratch_shapes=scratch,
        compiler_params=pltpu.CompilerParams(vmem_limit_bytes=16 << 20),
        cost_estimate=pl.CostEstimate(flops=flops, bytes_accessed=size, transcendentals=0),
    )(*args)


def chip_of(position, chips):
    return jnp.where(position < chips // 2, 2 * position, 2 * (chips - 1 - position) + 1)


def chip_at(chip, offset, chips):
    position = jnp.where(chip % 2 == 0, chip // 2, chips - 1 - chip // 2)
    return chip_of((position + offset + chips) % chips, chips)


def in_hbm(x):
    return pltpu.with_memory_space_constraint(x, pltpu.HBM)


def diagonal_of(weight):
    n = weight.shape[1]
    on = lax.broadcasted_iota(jnp.int32, (n, n), 0) == lax.broadcasted_iota(jnp.int32, (n, n), 1)
    return jnp.where(on, jnp.broadcast_to(weight, (n, n)), 0.0).astype(BF16)


def mask_body(table, rows, one, two, window, m_one, m_two, stack, weights, window_v, table_v, rows_v, one_v, two_v, sems):
    moves = (table, table_v), (rows, rows_v), (one, one_v), (two, two_v), (window, window_v)
    copies = [pltpu.make_async_copy(src, dst, sems.at[i]) for i, (src, dst) in enumerate(moves)]
    for copy in copies:
        copy.start()
    copies[0].wait()
    copies[1].wait()
    index = rows_v[...]
    n = one.shape[0]
    for which, panel, masked in ((0, one_v, m_one), (1, two_v, m_two)):
        weight = jnp.zeros(index.shape, F32)
        for s in range(table.shape[1]):
            weight = jnp.where(index == s, table_v[which, s].astype(F32), weight)
        weights[which : which + 1] = weight
        chosen = diagonal_of(weight)
        copies[2 + which].wait()
        value = dot(chosen, panel[...]).astype(BF16)
        masked[...] = value
        stack[which * n : (which + 1) * n] = value
    stack[2 * n :] = dot(diagonal_of(weights[0:1]), m_two[...]).astype(BF16)
    copies[4].wait()


def product(offset, window, swapped, piece):
    n = window.shape[0]
    me = lax.axis_index(AXIS)
    block = 2 * chip_at(me // 2, offset, window.shape[1] // (2 * n)) + me % 2
    columns = pl.ds(pl.multiple_of(block * n, n), n)
    value = piece[...]
    return dot(window[:, columns], value), dot(swapped[:, columns], value)


def plus(left, right, scale=1.0):
    return tuple(a + scale * b for a, b in zip(left, right, strict=True))


def add_products(total, chosen, window, swapped):
    for offset, piece in chosen:
        total = plus(total, product(offset, window, swapped, piece))
    return total


def early_body(window, swapped, one, up, down, two, back, *outs):
    zero = (jnp.zeros(one.shape, F32),) * 2
    own = product(0, window, swapped, one)
    side = plus(add_products(zero, up, window, swapped), own, 0.5)
    whole = plus(add_products(side, down, window, swapped), own, 0.5)
    own = product(0, window, swapped, two)
    side_two = plus(add_products(zero, back, window, swapped), own, 0.5)
    whole_two = plus(side_two, own, 0.5)
    for out, value in zip(outs, (*side, *whole, *side_two, *whole_two), strict=True):
        out[...] = value


def gram(stack, sibling, which, images):
    (a, b), (c, d) = halves(images[0]), halves(images[1])
    n = images[0].shape[0]
    mine, sibling = (x[which * n : (which + 1) * n] for x in (stack, sibling))
    return (dot_t(mine, a) + dot_t(sibling, c)) + (dot_t(mine, b) + dot_t(sibling, d))


def late_body(steps, window, swapped, *rest):
    sums, (stack, sibling, one, two), outs, parts = rest[:8], rest[8:12], rest[12:16], rest[16:]
    sums = [(sums[i][...], sums[i + 1][...]) for i in range(0, 8, 2)]
    far = product(-steps, window, swapped, one)
    image_one = plus(sums[1], far)
    first = gram(stack, sibling, 0, plus(sums[0], far, 0.5))
    far = product(steps, window, swapped, two)
    image_two = plus(sums[3], far)
    second = gram(stack, sibling, 1, plus(sums[2], far, 0.5))
    cross = -gram(stack, sibling, 2, image_one)
    for out, value in zip(outs, (*image_one, *image_two), strict=True):
        out[...] = value

    n = first.shape[0]
    half = n // 2
    row = lax.broadcasted_iota(jnp.int32, (n, n), 0)
    col = lax.broadcasted_iota(jnp.int32, (n, n), 1)
    second = second + second.T
    both = jnp.where(row <= col, first + first.T, second)
    diagonal = jnp.sum(jnp.where(row == col, second, 0.0), axis=0, keepdims=True)
    diagonal = jnp.broadcast_to(diagonal, (parts[0].shape[0] - half, n))
    low = lax.axis_index(AXIS) % 2 == 0
    for i, mine in enumerate((low, jnp.logical_not(low))):
        parts[i][:half] = jnp.where(mine, both[:half], both[half:])
        parts[i][half:] = diagonal
        parts[2 + i][...] = jnp.where(mine, cross[:half], cross[half:])


def rest_body(window, swapped, own_in, other_in, up, own, other):
    own[...], other[...] = add_products((own_in[...], other_in[...]), up, window, swapped)


def row_weights(weights, which):
    n = weights.shape[1]
    return dot(diagonal_of(weights[which : which + 1]), jnp.ones((n, n), BF16))


def columns_body(own_one, received_one, own_two, received_two, weights, cross, column_one, column_two):
    rounded = (-(row_weights(weights, 0) * (own_one[...] + received_one[...]))).astype(BF16)
    column_one[...] = rounded
    image = own_two[...] + received_two[...]
    column_two[...] = (-(row_weights(weights, 1) * (image + dot(rounded, cross[...])))).astype(BF16)


def last_body(pack_a, pack_b, cross_a, cross_b, cross, diag_one, diag_two, block_one, edge, block_two):
    n = cross.shape[0]
    half = n // 2
    first = lax.axis_index(AXIS) % 2 == 0

    def whole(a, b):
        return jnp.concatenate([jnp.where(first, a, b), jnp.where(first, b, a)], axis=0)

    row = lax.broadcasted_iota(jnp.int32, (n, n), 0)
    col = lax.broadcasted_iota(jnp.int32, (n, n), 1)
    packed = whole(pack_a[:half], pack_b[:half])
    turned = packed.T
    diagonal = jnp.where(first, pack_a[half : half + 1], pack_b[half : half + 1])
    s_one = jnp.where(row <= col, packed, turned)
    s_two = jnp.where(row > col, packed, turned)
    s_two = jnp.where(row == col, jnp.broadcast_to(diagonal, (n, n)), s_two)
    cross_sum = whole(cross_a[...], cross_b[...])
    c = cross[...]
    one = diag_one[...] + s_one
    block_one[...] = one
    a, b = halves(one)
    out = -(cross_sum.T + (dot(a, c) + dot(b, c)))
    edge[...] = out
    a, b = halves(out)
    d, e = halves(cross_sum)
    block_two[...] = diag_two[...] + s_two + (dot(d, c) + dot(e, c)) - (dot_t(c, a) + dot_t(c, b))


def local(
    inverse_window, panel_one, panel_two, cross_block, diag_one, diag_two, row_super, struct_mask, *, size
):
    chips = size // 2
    rows, width = panel_one.shape
    half = width // 2
    ring = [2 * r if r < chips // 2 else 2 * (chips - 1 - r) + 1 for r in range(chips)]
    ahead = [(2 * ring[r] + c, 2 * ring[(r + 1) % chips] + c) for r in range(chips) for c in (0, 1)]
    back = [(b, a) for a, b in ahead]
    flip = [[(i, i ^ (1 << b)) for i in range(size)] for b in range(size.bit_length() - 1)]

    def send(x, perm):
        return lax.ppermute(x, AXIS, perm)

    square = ((rows, width), F32)
    tile = ((rows, width), BF16)
    m_one, m_two, stack, weights, window = call(
        mask_body,
        "mask",
        (tile, tile, ((3 * rows, width), BF16), ((2, rows), F32), (inverse_window.shape, BF16)),
        tuple(map(in_hbm, (struct_mask, row_super.reshape(1, -1), panel_one, panel_two, inverse_window))),
        specs=[HBM] * 5,
        scratch=[
            pltpu.SMEM(struct_mask.shape, jnp.int32),
            pltpu.VMEM((1, rows), jnp.int32),
            pltpu.VMEM((rows, width), BF16),
            pltpu.VMEM((rows, width), BF16),
            pltpu.SemaphoreType.DMA((5,)),
        ],
    )

    steps = chips // 2
    one_up, one_down, two_up, two_down = [m_one], [m_one], [m_two], [m_two]
    for k in range(1, steps):
        one_up.append(send(one_up[-1], ahead))
        two_down.append(send(two_down[-1], back))
        one_down.append(send(one_down[-1], back))
        if k < steps - 1:
            two_up.append(send(two_up[-1], ahead))
    one_far = send(one_up[-1], ahead)
    two_far = send(two_down[-1], back)
    swapped = send(window, flip[0])
    sibling = send(stack, flip[0])

    def early_refs(*refs):
        inputs, outs = refs[: len(early_in)], refs[len(early_in) :]
        fixed, pieces = inputs[:2], inputs[2:]
        n = steps - 1
        one, up, down = pieces[0], pieces[1 : 1 + n], pieces[1 + n : 1 + 2 * n]
        two, behind = pieces[1 + 2 * n], pieces[2 + 2 * n :]
        early_body(
            *fixed,
            one,
            [(-k, p) for k, p in enumerate(up, 1)],
            [(k, p) for k, p in enumerate(down, 1)],
            two,
            [(k, p) for k, p in enumerate(behind, 1)],
            *outs,
        )

    one_up[-1], *_ = lax.optimization_barrier((one_up[-1], *two_up))
    early_in = (
        *(window, swapped),
        *one_up,
        *one_down[1:],
        *two_down,
    )
    block_flops = 4 * rows * width * width
    early = call(early_refs, "early", (square,) * 8, early_in, flops=block_flops * (3 * steps + 1))
    packed = ((half + 8, width), F32)
    crossed = ((half, width), F32)
    own_one, other_one, own_two, other_two, keep_p, away_p, keep_x, away_x = call(
        functools.partial(late_body, steps),
        "late",
        (square,) * 4 + (packed, packed, crossed, crossed),
        (window, swapped, *early, stack, sibling, one_far, two_far),
        flops=block_flops * 8,
    )
    pack_half = keep_p + send(away_p, flip[0])
    cross_half = keep_x + send(away_x, flip[0])
    pack_half, last_up = lax.optimization_barrier((pack_half, two_up[-1]))
    two_up.append(send(last_up, ahead))

    across = flip[1:]

    def summed(value, order):
        for perm in order:
            value = value.astype(BF16)
            value = value.astype(F32) + send(value, perm).astype(F32)
        return value

    pack_a = summed(pack_half, across)
    cross_a = summed(cross_half, across[1:] + across[:1])
    pack_b, cross_b = send(pack_a, flip[0]), send(cross_a, flip[0])

    received_one = send(other_one, flip[0])
    def rest_refs(*refs):
        inputs, outs = refs[: len(rest_in)], refs[len(rest_in) :]
        rest_body(*inputs[:4], [(-k, p) for k, p in enumerate(inputs[4:], 1)], *outs)

    rest_in = (window, swapped, own_two, other_two, *two_up[1:])
    own_two, other_two = call(rest_refs, "rest", (square,) * 2, rest_in, flops=block_flops * (steps - 1))
    received_two = send(other_two, flip[0])
    column_one, column_two = call(
        columns_body,
        "columns",
        (tile, tile),
        (own_one, received_one, own_two, received_two, weights, cross_block),
    )
    pack_b, column_two = lax.optimization_barrier((pack_b, column_two))
    full = ((width, width), F32)
    block_one, edge_block, block_two = call(
        last_body,
        "last",
        (full, full, full),
        (pack_a, pack_b, cross_a, cross_b, cross_block, diag_one, diag_two),
    )
    return column_one, block_one, column_two, edge_block, block_two


def solution(mesh):
    return jax.shard_map(
        functools.partial(local, size=mesh.shape[AXIS]),
        mesh=mesh,
        in_specs=(
            P(("pole", "prow"), None),
            P(("pole", "prow"), None),
            P(("pole", "prow"), None),
            P("pole", None),
            P("pole", None),
            P("pole", None),
            P("prow"),
            P(),
        ),
        out_specs=(
            P(("pole", "prow"), None),
            P("pole", None),
            P(("pole", "prow"), None),
            P("pole", None),
            P("pole", None),
        ),
        check_vma=False,
    )
```

```python
import functools

import jax
import jax.numpy as jnp
from jax import lax
from jax.experimental import pallas as pl
from jax.experimental.pallas import tpu as pltpu
from jax.sharding import PartitionSpec as P

F32, BF16 = jnp.float32, jnp.bfloat16
AXIS = "prow"
VMEM = pl.BlockSpec(memory_space=pltpu.VMEM)
SMEM = pl.BlockSpec(memory_space=pltpu.SMEM)
HBM = pl.BlockSpec(memory_space=pltpu.HBM)


def dot(left, right):
    return jnp.dot(left, right, preferred_element_type=F32)


def dot_t(left, right):
    return lax.dot_general(left, right, (((0,), (0,)), ((), ())), preferred_element_type=F32)


def halves(x):
    high = x.astype(BF16)
    return high, (x - high.astype(F32)).astype(BF16)


def call(body, name, outs, args, n_smem=0, flops=0, aliases=None, specs=None, scratch=(), out_spec=VMEM):
    size = sum(a.size * a.dtype.itemsize for a in args)
    return pl.pallas_call(
        body,
        name=name,
        out_shape=tuple(jax.ShapeDtypeStruct(s, d) for s, d in outs),
        in_specs=specs or [SMEM] * n_smem + [VMEM] * (len(args) - n_smem),
        out_specs=tuple(out_spec for _ in outs),
        input_output_aliases=aliases or {},
        scratch_shapes=scratch,
        compiler_params=pltpu.CompilerParams(vmem_limit_bytes=16 << 20),
        cost_estimate=pl.CostEstimate(flops=flops, bytes_accessed=size, transcendentals=0),
    )(*args)


def chip_of(position, chips):
    return jnp.where(position < chips // 2, 2 * position, 2 * (chips - 1 - position) + 1)


def chip_at(chip, offset, chips):
    position = jnp.where(chip % 2 == 0, chip // 2, chips - 1 - chip // 2)
    return chip_of((position + offset + chips) % chips, chips)


def in_hbm(x):
    return pltpu.with_memory_space_constraint(x, pltpu.HBM)


def load_body(window, out, sem):
    copy = pltpu.make_async_copy(window, out, sem)
    copy.start()
    copy.wait()


def diagonal_of(weight):
    n = weight.shape[1]
    on = lax.broadcasted_iota(jnp.int32, (n, n), 0) == lax.broadcasted_iota(jnp.int32, (n, n), 1)
    return jnp.where(on, jnp.broadcast_to(weight, (n, n)), 0.0).astype(BF16)


def mask_body(table, rows, one, two, m_one, m_two, stack, weights, table_v, rows_v, one_v, two_v, sems):
    moves = (table, table_v), (rows, rows_v), (one, one_v), (two, two_v)
    copies = [pltpu.make_async_copy(src, dst, sems.at[i]) for i, (src, dst) in enumerate(moves)]
    for copy in copies:
        copy.start()
    copies[0].wait()
    copies[1].wait()
    index = rows_v[...]
    n = one.shape[0]
    for which, panel, masked in ((0, one_v, m_one), (1, two_v, m_two)):
        weight = jnp.zeros(index.shape, F32)
        for s in range(table.shape[1]):
            weight = jnp.where(index == s, table_v[which, s].astype(F32), weight)
        weights[which : which + 1] = weight
        chosen = diagonal_of(weight)
        copies[2 + which].wait()
        value = dot(chosen, panel[...]).astype(BF16)
        masked[...] = value
        stack[which * n : (which + 1) * n] = value
    stack[2 * n :] = jnp.broadcast_to(weights[0:1], (stack.shape[0] - 2 * n, n)).astype(BF16)


def product(offset, window, swapped, piece):
    n = window.shape[0]
    me = lax.axis_index(AXIS)
    block = 2 * chip_at(me // 2, offset, window.shape[1] // (2 * n)) + me % 2
    columns = pl.ds(pl.multiple_of(block * n, n), n)
    value = piece[...]
    return dot(window[:, columns], value), dot(swapped[:, columns], value)


def plus(left, right, scale=1.0):
    return tuple(a + scale * b for a, b in zip(left, right, strict=True))


def add_products(total, chosen, window, swapped):
    for offset, piece in chosen:
        total = plus(total, product(offset, window, swapped, piece))
    return total


def early_body(window, swapped, stack, sibling, one, up, down, two, back, *outs):
    zero = (jnp.zeros(one.shape, F32),) * 2
    own = product(0, window, swapped, one)
    side = plus(add_products(zero, up, window, swapped), own, 0.5)
    whole = plus(add_products(side, down, window, swapped), own, 0.5)
    own = product(0, window, swapped, two)
    side_two = plus(add_products(zero, back, window, swapped), own, 0.5)
    whole_two = plus(side_two, own, 0.5)
    for out, value in zip(outs[:8], (*side, *whole, *side_two, *whole_two), strict=True):
        out[...] = value
    n = one.shape[0]
    for out, panel in zip(outs[8:], (stack, sibling), strict=True):
        weight = panel[2 * n :][:1].astype(F32)
        out[...] = dot(diagonal_of(weight), panel[n : 2 * n]).astype(BF16)


def gram(panels, images):
    (a, b), (c, d) = halves(images[0]), halves(images[1])
    mine, sibling = panels
    return (dot_t(mine, a) + dot_t(sibling, c)) + (dot_t(mine, b) + dot_t(sibling, d))


def late_body(steps, window, swapped, *rest):
    sums, twice, (stack, sibling, one, two), outs, parts = rest[:8], rest[8:10], rest[10:14], rest[14:18], rest[18:]
    sums = [(sums[i][...], sums[i + 1][...]) for i in range(0, 8, 2)]
    far = product(-steps, window, swapped, one)
    image_one = plus(sums[1], far)
    n = stack.shape[1]
    first = gram([x[:n] for x in (stack, sibling)], plus(sums[0], far, 0.5))
    far = product(steps, window, swapped, two)
    image_two = plus(sums[3], far)
    second = gram([x[n : 2 * n] for x in (stack, sibling)], plus(sums[2], far, 0.5))
    cross = -gram([x[...] for x in twice], image_one)
    for out, value in zip(outs, (*image_one, *image_two), strict=True):
        out[...] = value

    half = n // 2
    row = lax.broadcasted_iota(jnp.int32, (n, n), 0)
    col = lax.broadcasted_iota(jnp.int32, (n, n), 1)
    second = second + second.T
    both = jnp.where(row <= col, first + first.T, second)
    diagonal = jnp.sum(jnp.where(row == col, second, 0.0), axis=0, keepdims=True)
    diagonal = jnp.broadcast_to(diagonal, (parts[0].shape[0] - half, n))
    low = lax.axis_index(AXIS) % 2 == 0
    for i, mine in enumerate((low, jnp.logical_not(low))):
        parts[i][:half] = jnp.where(mine, both[:half], both[half:])
        parts[i][half:] = diagonal
        parts[2 + i][...] = jnp.where(mine, cross[:half], cross[half:])


def rest_body(window, swapped, own_in, other_in, up, own, other):
    own[...], other[...] = add_products((own_in[...], other_in[...]), up, window, swapped)


def row_weights(weights, which):
    n = weights.shape[1]
    return dot(diagonal_of(weights[which : which + 1]), jnp.ones((n, n), BF16))


def columns_body(own_one, received_one, own_two, received_two, weights, cross, column_one, column_two):
    rounded = (-(row_weights(weights, 0) * (own_one[...] + received_one[...]))).astype(BF16)
    column_one[...] = rounded
    image = own_two[...] + received_two[...]
    column_two[...] = (-(row_weights(weights, 1) * (image + dot(rounded, cross[...])))).astype(BF16)


def last_body(pack_a, pack_b, cross_a, cross_b, cross, diag_one, diag_two, block_one, edge, block_two, *held):
    n = cross.shape[0]
    half = n // 2
    first = lax.axis_index(AXIS) % 2 == 0

    def whole(a, b):
        return jnp.concatenate([jnp.where(first, a, b), jnp.where(first, b, a)], axis=0)

    row = lax.broadcasted_iota(jnp.int32, (n, n), 0)
    col = lax.broadcasted_iota(jnp.int32, (n, n), 1)
    packed = whole(pack_a[:half], pack_b[:half])
    turned = packed.T
    diagonal = jnp.where(first, pack_a[half : half + 1], pack_b[half : half + 1])
    s_one = jnp.where(row <= col, packed, turned)
    s_two = jnp.where(row > col, packed, turned)
    s_two = jnp.where(row == col, jnp.broadcast_to(diagonal, (n, n)), s_two)
    c = cross[...]
    *values, sems = held
    copies = [
        pltpu.make_async_copy(value, out, sems.at[i])
        for i, (value, out) in enumerate(zip(values, (block_one, edge, block_two), strict=True))
    ]

    one = diag_one[...] + s_one
    values[0][...] = one
    copies[0].start()
    a, b = halves(one)
    moved = dot(a, c) + dot(b, c)
    cross_sum = whole(cross_a[...], cross_b[...])
    values[1][...] = -(cross_sum.T + moved)
    copies[1].start()
    a, b = halves(moved)
    d, e = halves(cross_sum)
    bent = dot(d, c) + dot(e, c)
    values[2][...] = diag_two[...] + s_two + (bent + bent.T) + (dot_t(c, a) + dot_t(c, b))
    copies[2].start()
    for copy in copies:
        copy.wait()


def local(
    inverse_window, panel_one, panel_two, cross_block, diag_one, diag_two, row_super, struct_mask, *, size
):
    chips = size // 2
    rows, width = panel_one.shape
    half = width // 2
    ring = [2 * r if r < chips // 2 else 2 * (chips - 1 - r) + 1 for r in range(chips)]
    ahead = [(2 * ring[r] + c, 2 * ring[(r + 1) % chips] + c) for r in range(chips) for c in (0, 1)]
    back = [(b, a) for a, b in ahead]
    flip = [[(i, i ^ (1 << b)) for i in range(size)] for b in range(size.bit_length() - 1)]

    def send(x, perm):
        return lax.ppermute(x, AXIS, perm)

    square = ((rows, width), F32)
    tile = ((rows, width), BF16)
    m_one, m_two, stack, weights = call(
        mask_body,
        "mask",
        (tile, tile, ((2 * rows + 16, rows), BF16), ((2, rows), F32)),
        tuple(map(in_hbm, (struct_mask, row_super.reshape(1, -1), panel_one, panel_two))),
        specs=[HBM] * 4,
        scratch=[
            pltpu.SMEM(struct_mask.shape, jnp.int32),
            pltpu.VMEM((1, rows), jnp.int32),
            pltpu.VMEM((rows, width), BF16),
            pltpu.VMEM((rows, width), BF16),
            pltpu.SemaphoreType.DMA((4,)),
        ],
    )

    steps = chips // 2
    one_up, one_down, two_up, two_down = [m_one], [m_one], [m_two], [m_two]
    for k in range(1, steps):
        one_up.append(send(one_up[-1], ahead))
        two_down.append(send(two_down[-1], back))
        one_down.append(send(one_down[-1], back))
        if k < steps - 1:
            two_up.append(send(two_up[-1], ahead))
    one_far = send(one_up[-1], ahead)
    two_far = send(two_down[-1], back)
    late_window, *_ = lax.optimization_barrier((inverse_window, one_up[1], one_down[1], two_up[1], two_down[1]))
    (window,) = call(
        load_body,
        "load",
        ((inverse_window.shape, BF16),),
        (in_hbm(late_window),),
        specs=[HBM],
        scratch=[pltpu.SemaphoreType.DMA(())],
    )
    swapped = send(inverse_window, flip[0])
    sibling = send(stack, flip[0])

    def early_refs(*refs):
        inputs, outs = refs[: len(early_in)], refs[len(early_in) :]
        fixed, pieces = inputs[:4], inputs[4:]
        n = steps - 1
        one, up, down = pieces[0], pieces[1 : 1 + n], pieces[1 + n : 1 + 2 * n]
        two, behind = pieces[1 + 2 * n], pieces[2 + 2 * n :]
        early_body(
            *fixed,
            one,
            [(-k, p) for k, p in enumerate(up, 1)],
            [(k, p) for k, p in enumerate(down, 1)],
            two,
            [(k, p) for k, p in enumerate(behind, 1)],
            *outs,
        )

    one_up[-1], *_ = lax.optimization_barrier((one_up[-1], *two_up))
    early_in = (
        *(window, swapped, stack, sibling),
        *one_up,
        *one_down[1:],
        *two_down,
    )
    block_flops = 4 * rows * width * width
    early = call(early_refs, "early", (square,) * 8 + (tile,) * 2, early_in, flops=block_flops * (3 * steps + 1))
    packed = ((half + 8, width), F32)
    crossed = ((half, width), F32)
    own_one, other_one, own_two, other_two, keep_p, away_p, keep_x, away_x = call(
        functools.partial(late_body, steps),
        "late",
        (square,) * 4 + (packed, packed, crossed, crossed),
        (window, swapped, *early, stack, sibling, one_far, two_far),
        flops=block_flops * 8,
    )
    pack_half = keep_p + send(away_p, flip[0])
    cross_half = keep_x + send(away_x, flip[0])
    pack_half, last_up = lax.optimization_barrier((pack_half, two_up[-1]))
    two_up.append(send(last_up, ahead))

    across = flip[1:]

    def summed(value, order):
        for perm in order:
            value = value.astype(BF16)
            value = value.astype(F32) + send(value, perm).astype(F32)
        return value

    pack_a = summed(pack_half, across)
    cross_a = summed(cross_half, across[1:] + across[:1])
    pack_b, cross_b = send(pack_a, flip[0]), send(cross_a, flip[0])

    received_one = send(other_one, flip[0])
    def rest_refs(*refs):
        inputs, outs = refs[: len(rest_in)], refs[len(rest_in) :]
        rest_body(*inputs[:4], [(-k, p) for k, p in enumerate(inputs[4:], 1)], *outs)

    rest_in = (window, swapped, own_two, other_two, *two_up[1:])
    own_two, other_two = call(rest_refs, "rest", (square,) * 2, rest_in, flops=block_flops * (steps - 1))
    received_two = send(other_two, flip[0])
    column_one, column_two = call(
        columns_body,
        "columns",
        (tile, tile),
        (own_one, received_one, own_two, received_two, weights, cross_block),
    )
    pack_b, column_two = lax.optimization_barrier((pack_b, column_two))
    full = ((width, width), F32)
    block_one, edge_block, block_two = call(
        last_body,
        "last",
        (full, full, full),
        (pack_a, pack_b, cross_a, cross_b, cross_block, diag_one, diag_two),
        scratch=[pltpu.VMEM((width, width), F32)] * 3 + [pltpu.SemaphoreType.DMA((3,))],
        out_spec=HBM,
    )
    return column_one, block_one, column_two, edge_block, block_two


def solution(mesh):
    return jax.shard_map(
        functools.partial(local, size=mesh.shape[AXIS]),
        mesh=mesh,
        in_specs=(
            P(("pole", "prow"), None),
            P(("pole", "prow"), None),
            P(("pole", "prow"), None),
            P("pole", None),
            P("pole", None),
            P("pole", None),
            P("prow"),
            P(),
        ),
        out_specs=(
            P(("pole", "prow"), None),
            P("pole", None),
            P(("pole", "prow"), None),
            P("pole", None),
            P("pole", None),
        ),
        check_vma=False,
    )
```

```python
import functools

import jax
import jax.numpy as jnp
from jax import lax
from jax.experimental import pallas as pl
from jax.experimental.pallas import tpu as pltpu
from jax.sharding import PartitionSpec as P

F32, BF16 = jnp.float32, jnp.bfloat16
AXIS = "prow"
VMEM = pl.BlockSpec(memory_space=pltpu.VMEM)
SMEM = pl.BlockSpec(memory_space=pltpu.SMEM)
HBM = pl.BlockSpec(memory_space=pltpu.HBM)


def dot(left, right):
    return jnp.dot(left, right, preferred_element_type=F32)


def dot_t(left, right):
    return lax.dot_general(left, right, (((0,), (0,)), ((), ())), preferred_element_type=F32)


def halves(x):
    high = x.astype(BF16)
    return high, (x - high.astype(F32)).astype(BF16)


def call(body, name, outs, args, n_smem=0, flops=0, aliases=None, specs=None, scratch=(), out_spec=VMEM):
    size = sum(a.size * a.dtype.itemsize for a in args)
    return pl.pallas_call(
        body,
        name=name,
        out_shape=tuple(jax.ShapeDtypeStruct(s, d) for s, d in outs),
        in_specs=specs or [SMEM] * n_smem + [VMEM] * (len(args) - n_smem),
        out_specs=tuple(out_spec for _ in outs),
        input_output_aliases=aliases or {},
        scratch_shapes=scratch,
        compiler_params=pltpu.CompilerParams(vmem_limit_bytes=16 << 20),
        cost_estimate=pl.CostEstimate(flops=flops, bytes_accessed=size, transcendentals=0),
    )(*args)


def chip_of(position, chips):
    return jnp.where(position < chips // 2, 2 * position, 2 * (chips - 1 - position) + 1)


def chip_at(chip, offset, chips):
    position = jnp.where(chip % 2 == 0, chip // 2, chips - 1 - chip // 2)
    return chip_of((position + offset + chips) % chips, chips)


def in_hbm(x):
    return pltpu.with_memory_space_constraint(x, pltpu.HBM)


def load_body(window, out, sem):
    copy = pltpu.make_async_copy(window, out, sem)
    copy.start()
    copy.wait()


def diagonal_of(weight):
    n = weight.shape[1]
    on = lax.broadcasted_iota(jnp.int32, (n, n), 0) == lax.broadcasted_iota(jnp.int32, (n, n), 1)
    return jnp.where(on, jnp.broadcast_to(weight, (n, n)), 0.0).astype(BF16)


def mask_body(table, rows, one, two, m_one, m_two, stack, weights, table_v, rows_v, one_v, two_v, sems):
    moves = (table, table_v), (rows, rows_v), (one, one_v), (two, two_v)
    copies = [pltpu.make_async_copy(src, dst, sems.at[i]) for i, (src, dst) in enumerate(moves)]
    for copy in copies:
        copy.start()
    copies[0].wait()
    copies[1].wait()
    index = rows_v[...]
    n = one.shape[0]
    for which, panel, masked in ((0, one_v, m_one), (1, two_v, m_two)):
        weight = jnp.zeros(index.shape, F32)
        for s in range(table.shape[1]):
            weight = jnp.where(index == s, table_v[which, s].astype(F32), weight)
        weights[which : which + 1] = weight
        chosen = diagonal_of(weight)
        copies[2 + which].wait()
        value = dot(chosen, panel[...]).astype(BF16)
        masked[...] = value
        stack[which * n : (which + 1) * n] = value
    stack[2 * n :] = jnp.broadcast_to(weights[0:1], (stack.shape[0] - 2 * n, n)).astype(BF16)


def product(offset, window, swapped, piece):
    n = window.shape[0]
    me = lax.axis_index(AXIS)
    block = 2 * chip_at(me // 2, offset, window.shape[1] // (2 * n)) + me % 2
    columns = pl.ds(pl.multiple_of(block * n, n), n)
    value = piece[...]
    return dot(window[:, columns], value), dot(swapped[:, columns], value)


def plus(left, right, scale=1.0):
    return tuple(a + scale * b for a, b in zip(left, right, strict=True))


def add_products(total, chosen, window, swapped):
    for offset, piece in chosen:
        total = plus(total, product(offset, window, swapped, piece))
    return total


def early_body(window, swapped, stack, sibling, one, up, down, two, back, *outs):
    zero = (jnp.zeros(one.shape, F32),) * 2
    own = product(0, window, swapped, one)
    side = plus(add_products(zero, up, window, swapped), own, 0.5)
    whole = plus(add_products(side, down, window, swapped), own, 0.5)
    own = product(0, window, swapped, two)
    side_two = plus(add_products(zero, back, window, swapped), own, 0.5)
    whole_two = plus(side_two, own, 0.5)
    for out, value in zip(outs[:8], (*side, *whole, *side_two, *whole_two), strict=True):
        out[...] = value
    n = one.shape[0]
    for out, panel in zip(outs[8:], (stack, sibling), strict=True):
        weight = panel[2 * n :][:1].astype(F32)
        out[...] = dot(diagonal_of(weight), panel[n : 2 * n]).astype(BF16)


def gram(panels, images):
    both = jnp.concatenate(panels, axis=0)
    high, low = halves(jnp.concatenate(images, axis=0))
    return dot_t(both, high) + dot_t(both, low)


def late_body(steps, window, swapped, *rest):
    sums, twice, (stack, sibling, one, two), outs, parts = rest[:8], rest[8:10], rest[10:14], rest[14:18], rest[18:]
    sums = [(sums[i][...], sums[i + 1][...]) for i in range(0, 8, 2)]
    far = product(-steps, window, swapped, one)
    image_one = plus(sums[1], far)
    n = stack.shape[1]
    first = gram([x[:n] for x in (stack, sibling)], plus(sums[0], far, 0.5))
    far = product(steps, window, swapped, two)
    image_two = plus(sums[3], far)
    second = gram([x[n : 2 * n] for x in (stack, sibling)], plus(sums[2], far, 0.5))
    cross = -gram([x[...] for x in twice], image_one)
    for out, value in zip(outs, (*image_one, *image_two), strict=True):
        out[...] = value

    half = n // 2
    row = lax.broadcasted_iota(jnp.int32, (n, n), 0)
    col = lax.broadcasted_iota(jnp.int32, (n, n), 1)
    second = second + second.T
    both = jnp.where(row <= col, first + first.T, second)
    diagonal = jnp.sum(jnp.where(row == col, second, 0.0), axis=0, keepdims=True)
    diagonal = jnp.broadcast_to(diagonal, (parts[0].shape[0] - half, n))
    low = lax.axis_index(AXIS) % 2 == 0
    for i, mine in enumerate((low, jnp.logical_not(low))):
        parts[i][:half] = jnp.where(mine, both[:half], both[half:])
        parts[i][half:] = diagonal
        parts[2 + i][...] = jnp.where(mine, cross[:half], cross[half:])


def rest_body(window, swapped, own_in, other_in, up, own, other):
    own[...], other[...] = add_products((own_in[...], other_in[...]), up, window, swapped)


def row_weights(weights, which):
    n = weights.shape[1]
    return dot(diagonal_of(weights[which : which + 1]), jnp.ones((n, n), BF16))


def columns_body(own_one, received_one, own_two, received_two, weights, cross, column_one, column_two):
    rounded = (-(row_weights(weights, 0) * (own_one[...] + received_one[...]))).astype(BF16)
    column_one[...] = rounded
    image = own_two[...] + received_two[...]
    column_two[...] = (-(row_weights(weights, 1) * (image + dot(rounded, cross[...])))).astype(BF16)


def last_body(pack_a, pack_b, cross_a, cross_b, cross, diag_one, diag_two, block_one, edge, block_two, *held):
    n = cross.shape[0]
    half = n // 2
    first = lax.axis_index(AXIS) % 2 == 0

    def whole(a, b):
        return jnp.concatenate([jnp.where(first, a, b), jnp.where(first, b, a)], axis=0)

    row = lax.broadcasted_iota(jnp.int32, (n, n), 0)
    col = lax.broadcasted_iota(jnp.int32, (n, n), 1)
    packed = whole(pack_a[:half], pack_b[:half])
    turned = packed.T
    diagonal = jnp.where(first, pack_a[half : half + 1], pack_b[half : half + 1])
    s_one = jnp.where(row <= col, packed, turned)
    s_two = jnp.where(row > col, packed, turned)
    s_two = jnp.where(row == col, jnp.broadcast_to(diagonal, (n, n)), s_two)
    c = cross[...]
    *values, sems = held
    copies = [
        pltpu.make_async_copy(value, out, sems.at[i])
        for i, (value, out) in enumerate(zip(values, (block_one, edge, block_two), strict=True))
    ]

    one = diag_one[...] + s_one
    values[0][...] = one
    copies[0].start()
    a, b = halves(one)
    moved = dot(a, c) + dot(b, c)
    cross_sum = whole(cross_a[...], cross_b[...])
    values[1][...] = -(cross_sum.T + moved)
    copies[1].start()
    a, b = halves(moved)
    d, e = halves(cross_sum)
    bent = dot(d, c) + dot(e, c)
    values[2][...] = diag_two[...] + s_two + (bent + bent.T) + (dot_t(c, a) + dot_t(c, b))
    copies[2].start()
    for copy in copies:
        copy.wait()


def local(
    inverse_window, panel_one, panel_two, cross_block, diag_one, diag_two, row_super, struct_mask, *, size
):
    chips = size // 2
    rows, width = panel_one.shape
    half = width // 2
    ring = [2 * r if r < chips // 2 else 2 * (chips - 1 - r) + 1 for r in range(chips)]
    ahead = [(2 * ring[r] + c, 2 * ring[(r + 1) % chips] + c) for r in range(chips) for c in (0, 1)]
    back = [(b, a) for a, b in ahead]
    flip = [[(i, i ^ (1 << b)) for i in range(size)] for b in range(size.bit_length() - 1)]

    def send(x, perm):
        return lax.ppermute(x, AXIS, perm)

    square = ((rows, width), F32)
    tile = ((rows, width), BF16)
    m_one, m_two, stack, weights = call(
        mask_body,
        "mask",
        (tile, tile, ((2 * rows + 16, rows), BF16), ((2, rows), F32)),
        tuple(map(in_hbm, (struct_mask, row_super.reshape(1, -1), panel_one, panel_two))),
        specs=[HBM] * 4,
        scratch=[
            pltpu.SMEM(struct_mask.shape, jnp.int32),
            pltpu.VMEM((1, rows), jnp.int32),
            pltpu.VMEM((rows, width), BF16),
            pltpu.VMEM((rows, width), BF16),
            pltpu.SemaphoreType.DMA((4,)),
        ],
    )

    steps = chips // 2
    one_up, one_down, two_up, two_down = [m_one], [m_one], [m_two], [m_two]
    for k in range(1, steps):
        one_up.append(send(one_up[-1], ahead))
        two_down.append(send(two_down[-1], back))
        one_down.append(send(one_down[-1], back))
        if k < steps - 1:
            two_up.append(send(two_up[-1], ahead))
    one_far = send(one_up[-1], ahead)
    two_far = send(two_down[-1], back)
    late_window, *_ = lax.optimization_barrier((inverse_window, one_up[1], one_down[1], two_up[1], two_down[1]))
    (window,) = call(
        load_body,
        "load",
        ((inverse_window.shape, BF16),),
        (in_hbm(late_window),),
        specs=[HBM],
        scratch=[pltpu.SemaphoreType.DMA(())],
    )
    swapped = send(inverse_window, flip[0])
    sibling = send(stack, flip[0])

    def early_refs(*refs):
        inputs, outs = refs[: len(early_in)], refs[len(early_in) :]
        fixed, pieces = inputs[:4], inputs[4:]
        n = steps - 1
        one, up, down = pieces[0], pieces[1 : 1 + n], pieces[1 + n : 1 + 2 * n]
        two, behind = pieces[1 + 2 * n], pieces[2 + 2 * n :]
        early_body(
            *fixed,
            one,
            [(-k, p) for k, p in enumerate(up, 1)],
            [(k, p) for k, p in enumerate(down, 1)],
            two,
            [(k, p) for k, p in enumerate(behind, 1)],
            *outs,
        )

    one_up[-1], *_ = lax.optimization_barrier((one_up[-1], *two_up))
    early_in = (
        *(window, swapped, stack, sibling),
        *one_up,
        *one_down[1:],
        *two_down,
    )
    block_flops = 4 * rows * width * width
    early = call(early_refs, "early", (square,) * 8 + (tile,) * 2, early_in, flops=block_flops * (3 * steps + 1))
    packed = ((half + 8, width), F32)
    crossed = ((half, width), F32)
    own_one, other_one, own_two, other_two, keep_p, away_p, keep_x, away_x = call(
        functools.partial(late_body, steps),
        "late",
        (square,) * 4 + (packed, packed, crossed, crossed),
        (window, swapped, *early, stack, sibling, one_far, two_far),
        flops=block_flops * 8,
    )
    pack_half = keep_p + send(away_p, flip[0])
    cross_half = keep_x + send(away_x, flip[0])
    pack_half, last_up = lax.optimization_barrier((pack_half, two_up[-1]))
    two_up.append(send(last_up, ahead))

    across = flip[1:]

    def summed(value, order):
        for perm in order:
            value = value.astype(BF16)
            value = value.astype(F32) + send(value, perm).astype(F32)
        return value

    pack_a = summed(pack_half, across)
    cross_a = summed(cross_half, across[1:] + across[:1])
    pack_b, cross_b = send(pack_a, flip[0]), send(cross_a, flip[0])

    received_one = send(other_one, flip[0])
    def rest_refs(*refs):
        inputs, outs = refs[: len(rest_in)], refs[len(rest_in) :]
        rest_body(*inputs[:4], [(-k, p) for k, p in enumerate(inputs[4:], 1)], *outs)

    rest_in = (window, swapped, own_two, other_two, *two_up[1:])
    own_two, other_two = call(rest_refs, "rest", (square,) * 2, rest_in, flops=block_flops * (steps - 1))
    received_two = send(other_two, flip[0])
    column_one, column_two = call(
        columns_body,
        "columns",
        (tile, tile),
        (own_one, received_one, own_two, received_two, weights, cross_block),
    )
    pack_b, column_two = lax.optimization_barrier((pack_b, column_two))
    full = ((width, width), F32)
    block_one, edge_block, block_two = call(
        last_body,
        "last",
        (full, full, full),
        (pack_a, pack_b, cross_a, cross_b, cross_block, diag_one, diag_two),
        scratch=[pltpu.VMEM((width, width), F32)] * 3 + [pltpu.SemaphoreType.DMA((3,))],
        out_spec=HBM,
    )
    return column_one, block_one, column_two, edge_block, block_two


def solution(mesh):
    return jax.shard_map(
        functools.partial(local, size=mesh.shape[AXIS]),
        mesh=mesh,
        in_specs=(
            P(("pole", "prow"), None),
            P(("pole", "prow"), None),
            P(("pole", "prow"), None),
            P("pole", None),
            P("pole", None),
            P("pole", None),
            P("prow"),
            P(),
        ),
        out_specs=(
            P(("pole", "prow"), None),
            P("pole", None),
            P(("pole", "prow"), None),
            P("pole", None),
            P("pole", None),
        ),
        check_vma=False,
    )
```
